32 devices in a mesh: coil: 4 (over y, x), pencil: 8 (over z, core).
Axes of the slice: x: 2, y: 2, z: 4, core: 2. Of those that a mesh axis runs over, the one named last changes fastest.
Arguments:
- object_image: bfloat16 [32, 256, 1024], P(None, 'pencil'), may hold values from -6 to 6
- coil_maps: bfloat16 [64, 32, 256, 1024], P('coil', None, 'pencil'), may hold values from -0.75 to 0.75
- sample_mask: int32 [32, 256, 4], replicated, may hold values 0 or 1
Outputs:
- adjoint_image: float32 [32, 256, 1024], P('coil', 'pencil')
The draws below stay inside these ranges and needn't reach their ends.
Inputs may be any that keep to these rules, and one draw needn't show every extreme that they name: `sample_mask`: 1 where the 128 readout samples of a segment are acquired.
All inputs are finite; a program needn't handle non-finite values.
Results may differ from the reference program's by a relative error of at most 0.01.
Values may be sent and summed in bfloat16 or wider, within the bound.
A program may use at most 448 MiB of HBM per device.

```python
import math
import jax
import jax.numpy as jnp
from jax import lax

COILS = 64
SLICES = 32
NY = 256
NX = 512
SEG = 128


def touch_ends(result, key, least, largest):
    index_at = [jax.random.randint(jax.random.fold_in(key, axis), (), 0, length) for axis, length in enumerate(result.shape)]
    main_axis = result.shape.index(max(result.shape))
    neighbour = index_at[:main_axis] + [(index_at[main_axis] + 1) % result.shape[main_axis]] + index_at[main_axis + 1:]
    return result.at[tuple(index_at)].set(least).at[tuple(neighbour)].set(largest)


def block_scale(rng, dims, cuts, least, top_value):
    def one(axis_at, blocks):
        heights = jax.random.uniform(jax.random.fold_in(jax.random.fold_in(rng, 6), axis_at), (blocks,), jnp.float32, least / len(cuts), top_value / len(cuts))
        return jnp.repeat(jnp.exp(heights), dims[axis_at] // blocks).reshape((-1,) + (1,) * (len(dims) - axis_at - 1))

    level = one(*cuts[0])
    for cut in cuts[1:]:
        level = level * one(*cut)
    return level


def centred(rng, dims, width, most, split=(), kind=jnp.bfloat16):
    result = jax.random.normal(rng, dims, jnp.float32) * width
    if len(split) > 0:
        result = block_scale(rng, dims, split, -0.22, 0.18) * result
    return jnp.clip(result, min=-most, max=most).astype(kind)


def setup_inputs(seed: int = 0) -> dict:
    streams_of = jax.random.split(jax.random.key(seed), 4)
    object_image = centred(streams_of[0], (SLICES, NY, 2 * NX), 1.0, 6.0, ((1, 8),))
    coil_maps = centred(streams_of[1], (COILS, SLICES, NY, 2 * NX), COILS ** -0.5, 0.75, ((0, 4), (2, 8)))
    sample_mask = touch_ends((jax.random.randint(streams_of[2], (SLICES, NY, NX // SEG), 0, 2) < 1).astype(jnp.int32), jax.random.fold_in(streams_of[2], 1), 0, 1)
    return {"object_image": object_image, "coil_maps": coil_maps, "sample_mask": sample_mask}


def dft_tables(length, direction):
    indices = jnp.arange(length, dtype=jnp.int32)
    phases = indices[:, None] * indices[None, :] % length
    angles = phases.astype(jnp.float32) * (2.0 * math.pi / length)
    factor = 1.0 / math.sqrt(length)
    cosine = (jnp.cos(angles) * factor).astype(jnp.bfloat16)
    sine_part = (direction * jnp.sin(angles) * factor).astype(jnp.bfloat16)
    return (cosine, sine_part)

def readout_table(length, direction):
    cosine, sine_part = dft_tables(length, direction)
    upper = jnp.concatenate([cosine, sine_part], axis=1)
    lower = jnp.concatenate([-sine_part, cosine], axis=1)
    return jnp.concatenate([upper, lower], axis=0)

def complex_product(left_side, right_side, readout, conjugate):
    left_full = left_side.astype(jnp.float32)
    right_full = right_side.astype(jnp.float32)
    left_real = left_full[..., :readout]
    left_imag = left_full[..., readout:]
    if conjugate:
        left_imag = -left_imag
    right_real = right_full[..., :readout]
    right_imag = right_full[..., readout:]
    real_part = left_real * right_real - left_imag * right_imag
    imag_part = left_real * right_imag + left_imag * right_real
    return jnp.concatenate([real_part, imag_part], axis=-1)

def transform(volume, tables, formula, readout):
    cosine, sine_part = tables
    volume_full = volume.astype(jnp.float32)
    direct = jnp.einsum(formula, cosine.astype(jnp.float32), volume_full)
    crossed = jnp.einsum(formula, sine_part.astype(jnp.float32), volume_full)
    turned = jnp.concatenate([-crossed[..., readout:], crossed[..., :readout]], axis=-1)
    return (direct + turned).astype(jnp.bfloat16)

def widen(mask_part, segment):
    flags = jnp.repeat(mask_part, segment, axis=2) > 0
    return jnp.concatenate([flags, flags], axis=2)

def reference(object_image, coil_maps, sample_mask):
    readout = NX
    forward_x = readout_table(NX, -1.0).astype(jnp.float32)
    inverse_x = readout_table(NX, 1.0).astype(jnp.float32)
    forward_z = dft_tables(SLICES, -1.0)
    inverse_z = dft_tables(SLICES, 1.0)
    forward_y = dft_tables(NY, -1.0)
    inverse_y = dft_tables(NY, 1.0)
    sampled_cells = widen(sample_mask, SEG)

    def one_coil(summed, coil_map):
        coil_image = complex_product(coil_map, object_image, readout, False).astype(jnp.bfloat16)
        volume = jnp.dot(coil_image.astype(jnp.float32), forward_x, precision=lax.Precision.HIGHEST).astype(jnp.bfloat16)
        volume = transform(volume, forward_z, 'kz,zyx->kyx', readout)
        volume = transform(volume, forward_y, 'ky,zyx->zkx', readout)
        volume = jnp.where(sampled_cells, volume, jnp.zeros_like(volume))
        volume = transform(volume, inverse_y, 'ky,zyx->zkx', readout)
        volume = transform(volume, inverse_z, 'kz,zyx->kyx', readout)
        volume = jnp.dot(volume.astype(jnp.float32), inverse_x, precision=lax.Precision.HIGHEST).astype(jnp.bfloat16)
        return (summed + complex_product(coil_map, volume, readout, True), None)
    start = jnp.zeros((SLICES, NY, 2 * NX), jnp.float32)
    summed, unused = lax.scan(one_coil, start, coil_maps)
    return summed
```

```python
import math

import jax
import jax.numpy as jnp
from jax import lax
from jax.experimental import pallas as pl
from jax.experimental.pallas import tpu as pltpu
from jax.sharding import PartitionSpec as P


def dft_tables(length, direction):
    indices = jnp.arange(length, dtype=jnp.int32)
    phases = indices[:, None] * indices[None, :] % length
    angles = phases.astype(jnp.float32) * (2.0 * math.pi / length)
    factor = 1.0 / math.sqrt(length)
    cosine = (jnp.cos(angles) * factor).astype(jnp.bfloat16)
    sine_part = (direction * jnp.sin(angles) * factor).astype(jnp.bfloat16)
    return (cosine, sine_part)


def readout_table(length, direction):
    cosine, sine_part = dft_tables(length, direction)
    upper = jnp.concatenate([cosine, sine_part], axis=1)
    lower = jnp.concatenate([-sine_part, cosine], axis=1)
    return jnp.concatenate([upper, lower], axis=0)


def complex_product(left_side, right_side, readout, conjugate):
    left_full = left_side.astype(jnp.float32)
    right_full = right_side.astype(jnp.float32)
    left_real = left_full[..., :readout]
    left_imag = left_full[..., readout:]
    if conjugate:
        left_imag = -left_imag
    right_real = right_full[..., :readout]
    right_imag = right_full[..., readout:]
    real_part = left_real * right_real - left_imag * right_imag
    imag_part = left_real * right_imag + left_imag * right_real
    return jnp.concatenate([real_part, imag_part], axis=-1)


def transform(volume, tables, formula, readout):
    cosine, sine_part = tables
    direct = jnp.einsum(formula, cosine, volume, preferred_element_type=jnp.float32)
    crossed = jnp.einsum(formula, sine_part, volume, preferred_element_type=jnp.float32)
    turned = jnp.concatenate([-crossed[..., readout:], crossed[..., :readout]], axis=-1)
    return (direct + turned).astype(jnp.bfloat16)


def widen(mask_part, segment):
    flags = jnp.repeat(mask_part, segment, axis=2) > 0
    return jnp.concatenate([flags, flags], axis=2)


def split_lines(object_image, coil_maps, sample_mask):
    readout = object_image.shape[2] // 2
    slices = object_image.shape[0]
    row_count = object_image.shape[1]
    pencils = lax.axis_size("pencil")
    depth = slices // pencils
    lines = row_count * pencils
    segment = readout // sample_mask.shape[2]
    position = lax.axis_index("pencil")
    forward_x = readout_table(readout, -1.0)
    inverse_x = readout_table(readout, 1.0)
    forward_z = dft_tables(slices, -1.0)
    inverse_z = dft_tables(slices, 1.0)
    forward_y = dft_tables(lines, -1.0)
    inverse_y = dft_tables(lines, 1.0)
    column_mask = widen(lax.dynamic_slice_in_dim(sample_mask, position * depth, depth, 0), segment)
    nothing = jnp.zeros((), jnp.bfloat16)
    coil_image = complex_product(coil_maps, object_image[None], readout, False).astype(jnp.bfloat16)
    volume = jnp.dot(coil_image, forward_x, preferred_element_type=jnp.float32).astype(jnp.bfloat16)
    volume = transform(volume, forward_z, "kz,czyx->ckyx", readout)
    spectrum = transform(
        lax.all_to_all(volume, "pencil", split_axis=1, concat_axis=2, tiled=True),
        forward_y,
        "ky,czyx->czkx",
        readout,
    )
    spectrum = jnp.where(column_mask, spectrum, nothing)
    spectrum = transform(spectrum, inverse_y, "ky,czyx->czkx", readout)
    coil_block = lax.all_to_all(spectrum, "pencil", split_axis=2, concat_axis=1, tiled=True)
    coil_block = transform(coil_block, inverse_z, "kz,czyx->ckyx", readout)
    returned = jnp.dot(coil_block, inverse_x, preferred_element_type=jnp.float32).astype(
        jnp.bfloat16
    )
    partial_sum = jnp.sum(complex_product(coil_maps, returned, readout, True), axis=0)
    return lax.psum_scatter(
        partial_sum.astype(jnp.bfloat16), "coil", scatter_dimension=0, tiled=True
    ).astype(jnp.float32)


MESH = pl.DeviceIdType.MESH


def rotation(cosine, sine_part, rows):
    if rows:
        upper = jnp.concatenate([cosine, sine_part], axis=1)
        lower = jnp.concatenate([-sine_part, cosine], axis=1)
    else:
        upper = jnp.concatenate([cosine, -sine_part], axis=1)
        lower = jnp.concatenate([sine_part, cosine], axis=1)
    return jnp.concatenate([upper, lower], axis=0)


def plan_tables(slices, lines, readout, group):
    eye = jnp.eye(group, dtype=jnp.bfloat16)
    quarter, half_y, half_z = readout // 4, lines // 2, slices // 2
    cx, sx = dft_tables(readout, -1.0)
    x_fwd = jnp.stack([rotation(cx[:quarter, r::4], sx[:quarter, r::4], True) for r in range(4)])
    cx, sx = dft_tables(readout, 1.0)
    x_inv = jnp.stack([rotation(cx[r::4, :quarter], sx[r::4, :quarter], True) for r in range(4)])
    cy, sy = dft_tables(lines, -1.0)
    y_fwd = jnp.stack([rotation(cy[p::2, :half_y], sy[p::2, :half_y], False) for p in range(2)])
    cy, sy = dft_tables(lines, 1.0)
    y_inv = jnp.stack([rotation(cy[:half_y, p::2], sy[:half_y, p::2], False) for p in range(2)])
    cz, sz = dft_tables(slices, -1.0)
    z_fwd = jnp.stack(
        [
            rotation(jnp.kron(cz[p::2, :half_z], eye), jnp.kron(sz[p::2, :half_z], eye), False)
            for p in range(2)
        ]
    )
    cz, sz = dft_tables(slices, 1.0)
    z_inv = jnp.stack(
        [
            rotation(jnp.kron(cz[:half_z, p::2], eye), jnp.kron(sz[:half_z, p::2], eye), False)
            for p in range(2)
        ]
    )
    return x_fwd, x_inv, y_fwd, y_inv, z_fwd, z_inv


def mm(left, right):
    return jnp.dot(left, right, preferred_element_type=jnp.float32)


def forward_body(map_part, image_part, x_fwd, y_fwd):
    lines = map_part.shape[0]
    readout = map_part.shape[1] // 2
    quarter, half = readout // 4, lines // 2
    left = map_part.astype(jnp.float32)
    right = image_part.astype(jnp.float32)
    re, im = [], []
    for q in range(4):
        a, b = q * quarter, (q + 1) * quarter
        lr, li = left[:, a:b], left[:, readout + a : readout + b]
        rr, ri = right[:, a:b], right[:, readout + a : readout + b]
        re.append(lr * rr - li * ri)
        im.append(lr * ri + li * rr)
    sum_re, sum_im = re[0] + re[2], im[0] + im[2]
    dif_re, dif_im = re[0] - re[2], im[0] - im[2]
    odd_re, odd_im = re[1] + re[3], im[1] + im[3]
    tur_re, tur_im = re[1] - re[3], im[1] - im[3]
    mixed = [
        (sum_re + odd_re, sum_im + odd_im),
        (dif_re + tur_im, dif_im - tur_re),
        (sum_re - odd_re, sum_im - odd_im),
        (dif_re - tur_im, dif_im + tur_re),
    ]
    even, odd = [], []
    for r in range(4):
        v = mm(jnp.concatenate(mixed[r], axis=1).astype(jnp.bfloat16), x_fwd[r])
        e = (v[:half] + v[half:]).astype(jnp.bfloat16)
        o = (v[:half] - v[half:]).astype(jnp.bfloat16)
        even.append(jnp.concatenate([e[:, :quarter], e[:, quarter:]], axis=0))
        odd.append(jnp.concatenate([o[:, :quarter], o[:, quarter:]], axis=0))
    even = mm(y_fwd[0], jnp.concatenate(even, axis=1)).astype(jnp.bfloat16)
    odd = mm(y_fwd[1], jnp.concatenate(odd, axis=1)).astype(jnp.bfloat16)
    return even, odd


def slab_body(block, mask_block, z_fwd, z_inv):
    slices, group, width = block.shape
    half, readout = slices // 2, width // 2
    flat = half * group
    low = block[:half].astype(jnp.float32)
    high = block[half:].astype(jnp.float32)
    parts = [low + high, low - high]
    back = []
    for p in range(2):
        u = parts[p].astype(jnp.bfloat16).reshape(flat, width)
        u = jnp.concatenate([u[:, :readout], u[:, readout:]], axis=0)
        k = mm(z_fwd[p], u)
        m = mask_block[p].reshape(flat, readout).astype(jnp.float32)
        k = jnp.concatenate([k[:flat] * m, k[flat:] * m], axis=0).astype(jnp.bfloat16)
        back.append(mm(z_inv[p], k))

    def place(t):
        t = t.astype(jnp.bfloat16)
        return jnp.concatenate([t[:flat], t[flat:]], axis=1).reshape(half, group, width)

    return place(back[0] + back[1]), place(back[0] - back[1])


def backward_body(block, map_part, x_inv, y_inv):
    lines = block.shape[0]
    readout = block.shape[1] // 2
    quarter, half = readout // 4, lines // 2
    sides = []
    for p in range(2):
        part = block[p * half : (p + 1) * half]
        sides.append(mm(y_inv[p], jnp.concatenate([part[:, :readout], part[:, readout:]], axis=0)))
    lows = (sides[0] + sides[1]).astype(jnp.bfloat16)
    highs = (sides[0] - sides[1]).astype(jnp.bfloat16)
    t_re, t_im = [], []
    for r in range(4):
        a, b = r * quarter, (r + 1) * quarter
        rows = jnp.concatenate(
            [
                jnp.concatenate([lows[:half, a:b], lows[half:, a:b]], axis=1),
                jnp.concatenate([highs[:half, a:b], highs[half:, a:b]], axis=1),
            ],
            axis=0,
        )
        t = mm(rows, x_inv[r])
        t_re.append(t[:, :quarter])
        t_im.append(t[:, quarter:])
    sr, si = t_re[0] + t_re[2], t_im[0] + t_im[2]
    dr, di = t_re[0] - t_re[2], t_im[0] - t_im[2]
    er, ei = t_re[1] + t_re[3], t_im[1] + t_im[3]
    fr, fi = t_re[1] - t_re[3], t_im[1] - t_im[3]
    image = [(sr + er, si + ei), (dr - fi, di + fr), (sr - er, si - ei), (dr + fi, di - fr)]
    maps = map_part.astype(jnp.float32)
    out_re, out_im = [], []
    for q in range(4):
        a, b = q * quarter, (q + 1) * quarter
        mr, mi = maps[:, a:b], maps[:, readout + a : readout + b]
        xr, xi = image[q]
        out_re.append(mr * xr + mi * xi)
        out_im.append(mr * xi - mi * xr)
    return jnp.concatenate(out_re + out_im, axis=1)


def image_rows(image_ref):
    chips = image_ref.shape[2]
    return jnp.concatenate([image_ref[i % 2, 0, i // 2] for i in range(2 * chips)], axis=0)


def forward_call(maps, image, x_fwd, y_fwd):
    coils, slices, lines, width = maps.shape
    chips, rows = image.shape[2], image.shape[3]
    half = lines // 2

    def body(map_ref, image_ref, x_ref, y_ref, out_ref):
        even, odd = forward_body(map_ref[0, 0], image_rows(image_ref), x_ref[...], y_ref[...])
        readout = even.shape[1]
        out_ref[0, 0, :half, :readout] = even[:half]
        out_ref[0, 0, :half, readout:] = even[half:]
        out_ref[0, 0, half:, :readout] = odd[:half]
        out_ref[0, 0, half:, readout:] = odd[half:]

    return pl.pallas_call(
        body,
        grid=(slices, coils),
        out_shape=jax.ShapeDtypeStruct(maps.shape, jnp.bfloat16),
        in_specs=[
            pl.BlockSpec((1, 1, lines, width), lambda z, j: (j, z, 0, 0)),
            pl.BlockSpec((2, 1, chips, rows, width), lambda z, j: (0, z, 0, 0, 0)),
            pl.BlockSpec(x_fwd.shape, lambda z, j: (0, 0, 0)),
            pl.BlockSpec(y_fwd.shape, lambda z, j: (0, 0, 0)),
        ],
        out_specs=pl.BlockSpec((1, 1, lines, width), lambda z, j: (j, z, 0, 0)),
        compiler_params=pltpu.CompilerParams(vmem_limit_bytes=48 << 20),
        name="forward_xy",
    )(maps, image, x_fwd, y_fwd)


def slab_call(volume, mask, z_fwd, z_inv, group):
    coils, slices, lines, width = volume.shape
    half = slices // 2

    def body(block_ref, mask_ref, f_ref, b_ref, out_ref):
        low, high = slab_body(block_ref[0], mask_ref[...], f_ref[...], b_ref[...])
        out_ref[0, :half] = low
        out_ref[0, half:] = high

    return pl.pallas_call(
        body,
        grid=(lines // group, coils),
        out_shape=jax.ShapeDtypeStruct(volume.shape, jnp.bfloat16),
        in_specs=[
            pl.BlockSpec((1, slices, group, width), lambda y, j: (j, 0, y, 0)),
            pl.BlockSpec((2, half, group, width // 2), lambda y, j: (0, 0, y, 0)),
            pl.BlockSpec(z_fwd.shape, lambda y, j: (0, 0, 0)),
            pl.BlockSpec(z_inv.shape, lambda y, j: (0, 0, 0)),
        ],
        out_specs=pl.BlockSpec((1, slices, group, width), lambda y, j: (j, 0, y, 0)),
        compiler_params=pltpu.CompilerParams(vmem_limit_bytes=48 << 20),
        name="slab_mask",
    )(volume, mask, z_fwd, z_inv)


def backward_call(volume, maps, x_inv, y_inv):
    coils, slices, lines, width = volume.shape

    def body(block_ref, map_ref, x_ref, y_ref, out_ref):
        total = backward_body(block_ref[0, 0], map_ref[0, 0], x_ref[...], y_ref[...])
        for j in range(1, coils):
            total += backward_body(block_ref[j, 0], map_ref[j, 0], x_ref[...], y_ref[...])
        out_ref[0] = total.astype(out_ref.dtype)

    return pl.pallas_call(
        body,
        grid=(slices,),
        out_shape=jax.ShapeDtypeStruct((slices, lines, width), jnp.bfloat16),
        in_specs=[
            pl.BlockSpec((coils, 1, lines, width), lambda z: (0, z, 0, 0)),
            pl.BlockSpec((coils, 1, lines, width), lambda z: (0, z, 0, 0)),
            pl.BlockSpec(x_inv.shape, lambda z: (0, 0, 0)),
            pl.BlockSpec(y_inv.shape, lambda z: (0, 0, 0)),
        ],
        out_specs=pl.BlockSpec((1, lines, width), lambda z: (z, 0, 0)),
        compiler_params=pltpu.CompilerParams(vmem_limit_bytes=56 << 20),
        name="backward_yx",
    )(volume, maps, x_inv, y_inv)


def exchange_call(coil_maps, object_image):
    pencils, columns = lax.axis_size("pencil"), lax.axis_size("coil")
    coils, slices, rows, width = coil_maps.shape
    per, chips, share = coils // pencils, pencils // 2, slices // columns
    shifts = sorted(range(1, pencils), key=lambda s: abs(s - pencils // 2))

    def kernel(
        map_ref, image_ref, out_ref, full_ref, own_sem, map_send, map_recv, im_send, im_recv,
        col_send, col_recv, core_send, core_recv,
    ):
        me, column = lax.axis_index("pencil"), lax.axis_index("coil")
        chip, core = me // 2, me % 2

        barrier = pltpu.get_barrier_semaphore()
        for s in range(1, pencils):
            pl.semaphore_signal(
                barrier, device_id=(column, lax.rem(me + s, pencils)), device_id_type=MESH
            )
        for s in range(1, columns):
            pl.semaphore_signal(
                barrier, device_id=(lax.rem(column + s, columns), me), device_id_type=MESH
            )
        pl.semaphore_wait(barrier, pencils + columns - 2)

        quarter = pl.ds(column * share, share)
        own = [
            pltpu.make_async_copy(
                image_ref.at[quarter], full_ref.at[core, quarter, chip], own_sem.at[per]
            )
        ]
        for j in range(per):
            own.append(
                pltpu.make_async_copy(
                    map_ref.at[me * per + j], out_ref.at[j, :, pl.ds(me * rows, rows)], own_sem.at[j]
                )
            )
        along = []
        for i, s in enumerate(range(1, chips)):
            along.append(
                pltpu.make_async_remote_copy(
                    src_ref=image_ref.at[quarter],
                    dst_ref=full_ref.at[core, quarter, chip],
                    send_sem=im_send.at[i],
                    recv_sem=im_recv.at[i],
                    device_id=(column, lax.rem(me + 2 * s, pencils)),
                    device_id_type=MESH,
                )
            )
        moves = []
        for j in range(per):
            for i, s in enumerate(shifts):
                target = lax.rem(me + s, pencils)
                moves.append(
                    pltpu.make_async_remote_copy(
                        src_ref=map_ref.at[target * per + j],
                        dst_ref=out_ref.at[j, :, pl.ds(me * rows, rows)],
                        send_sem=map_send.at[j, i],
                        recv_sem=map_recv.at[j, i],
                        device_id=(column, target),
                        device_id_type=MESH,
                    )
                )
        for copy in along + moves + own:
            copy.start()
        own[0].wait()
        for copy in along:
            copy.wait()
        across = []
        for i, s in enumerate(range(1, columns)):
            across.append(
                pltpu.make_async_remote_copy(
                    src_ref=full_ref.at[core, quarter],
                    dst_ref=full_ref.at[core, quarter],
                    send_sem=col_send.at[i],
                    recv_sem=col_recv.at[i],
                    device_id=(lax.rem(column + s, columns), me),
                    device_id_type=MESH,
                )
            )
        for copy in across:
            copy.start()
        for copy in across:
            copy.wait()
        pair = pltpu.make_async_remote_copy(
            src_ref=full_ref.at[core],
            dst_ref=full_ref.at[core],
            send_sem=core_send,
            recv_sem=core_recv,
            device_id=(column, me + 1 - 2 * core),
            device_id_type=MESH,
        )
        pair.start()
        pair.wait()
        for copy in own[1:] + moves:
            copy.wait()

    dma = pltpu.SemaphoreType.DMA
    anywhere = pl.BlockSpec(memory_space=pl.ANY)
    return pl.pallas_call(
        kernel,
        out_shape=[
            jax.ShapeDtypeStruct((per, slices, rows * pencils, width), jnp.bfloat16),
            jax.ShapeDtypeStruct((2, slices, chips, rows, width), jnp.bfloat16),
        ],
        in_specs=[anywhere, anywhere],
        out_specs=[anywhere, anywhere],
        scratch_shapes=[
            dma((per + 1,)),
            dma((per, pencils - 1)),
            dma((per, pencils - 1)),
            dma((chips - 1,)),
            dma((chips - 1,)),
            dma((columns - 1,)),
            dma((columns - 1,)),
            dma,
            dma,
        ],
        compiler_params=pltpu.CompilerParams(collective_id=0, has_side_effects=True),
        name="exchange_maps",
    )(coil_maps, object_image)


def plan_mask(sample_mask, readout):
    slices, lines, segments = sample_mask.shape
    run = readout // segments // 4
    flags = sample_mask.reshape(slices // 2, 2, lines // 2, 2, segments).transpose(1, 0, 3, 2, 4)
    flags = (flags > 0).astype(jnp.bfloat16).reshape(2, slices // 2, lines, segments)
    return jnp.tile(jnp.repeat(flags, run, axis=3), (1, 1, 1, 4))


def whole_coils(object_image, coil_maps, sample_mask):
    readout = object_image.shape[2] // 2
    slices = object_image.shape[0]
    lines = object_image.shape[1] * lax.axis_size("pencil")
    group = 16
    x_fwd, x_inv, y_fwd, y_inv, z_fwd, z_inv = plan_tables(slices, lines, readout, group)
    mask = plan_mask(sample_mask, readout)
    maps, image = exchange_call(coil_maps, object_image)
    volume = forward_call(maps, image, x_fwd, y_fwd)
    volume = slab_call(volume, mask, z_fwd, z_inv, group)
    partial_sum = backward_call(volume, maps, x_inv, y_inv)
    partial_sum = lax.psum_scatter(partial_sum, "coil", scatter_dimension=0, tiled=True)
    return lax.psum_scatter(partial_sum, "pencil", scatter_dimension=1, tiled=True).astype(
        jnp.float32
    )


def solution(mesh):
    placed = (P(None, "pencil", None), P("coil", None, "pencil", None), P())

    def on_device(object_image, coil_maps, sample_mask):
        whole = coil_maps.shape[0] % lax.axis_size("pencil") == 0
        return (whole_coils if whole else split_lines)(object_image, coil_maps, sample_mask)

    return jax.shard_map(
        on_device, mesh=mesh, in_specs=placed, out_specs=P("coil", "pencil", None), check_vma=False
    )
```

```python
import math

import numpy as np

import jax
import jax.numpy as jnp
from jax import lax
from jax.experimental import pallas as pl
from jax.experimental.pallas import tpu as pltpu
from jax.sharding import PartitionSpec as P


def dft_tables(length, direction):
    indices = jnp.arange(length, dtype=jnp.int32)
    phases = indices[:, None] * indices[None, :] % length
    angles = phases.astype(jnp.float32) * (2.0 * math.pi / length)
    factor = 1.0 / math.sqrt(length)
    cosine = (jnp.cos(angles) * factor).astype(jnp.bfloat16)
    sine_part = (direction * jnp.sin(angles) * factor).astype(jnp.bfloat16)
    return (cosine, sine_part)


def readout_table(length, direction):
    cosine, sine_part = dft_tables(length, direction)
    upper = jnp.concatenate([cosine, sine_part], axis=1)
    lower = jnp.concatenate([-sine_part, cosine], axis=1)
    return jnp.concatenate([upper, lower], axis=0)


def complex_product(left_side, right_side, readout, conjugate):
    left_full = left_side.astype(jnp.float32)
    right_full = right_side.astype(jnp.float32)
    left_real = left_full[..., :readout]
    left_imag = left_full[..., readout:]
    if conjugate:
        left_imag = -left_imag
    right_real = right_full[..., :readout]
    right_imag = right_full[..., readout:]
    real_part = left_real * right_real - left_imag * right_imag
    imag_part = left_real * right_imag + left_imag * right_real
    return jnp.concatenate([real_part, imag_part], axis=-1)


def transform(volume, tables, formula, readout):
    cosine, sine_part = tables
    direct = jnp.einsum(formula, cosine, volume, preferred_element_type=jnp.float32)
    crossed = jnp.einsum(formula, sine_part, volume, preferred_element_type=jnp.float32)
    turned = jnp.concatenate([-crossed[..., readout:], crossed[..., :readout]], axis=-1)
    return (direct + turned).astype(jnp.bfloat16)


def widen(mask_part, segment):
    flags = jnp.repeat(mask_part, segment, axis=2) > 0
    return jnp.concatenate([flags, flags], axis=2)


def split_lines(object_image, coil_maps, sample_mask):
    readout = object_image.shape[2] // 2
    slices = object_image.shape[0]
    row_count = object_image.shape[1]
    pencils = lax.axis_size("pencil")
    depth = slices // pencils
    lines = row_count * pencils
    segment = readout // sample_mask.shape[2]
    position = lax.axis_index("pencil")
    forward_x = readout_table(readout, -1.0)
    inverse_x = readout_table(readout, 1.0)
    forward_z = dft_tables(slices, -1.0)
    inverse_z = dft_tables(slices, 1.0)
    forward_y = dft_tables(lines, -1.0)
    inverse_y = dft_tables(lines, 1.0)
    column_mask = widen(lax.dynamic_slice_in_dim(sample_mask, position * depth, depth, 0), segment)
    nothing = jnp.zeros((), jnp.bfloat16)
    coil_image = complex_product(coil_maps, object_image[None], readout, False).astype(jnp.bfloat16)
    volume = jnp.dot(coil_image, forward_x, preferred_element_type=jnp.float32).astype(jnp.bfloat16)
    volume = transform(volume, forward_z, "kz,czyx->ckyx", readout)
    spectrum = transform(
        lax.all_to_all(volume, "pencil", split_axis=1, concat_axis=2, tiled=True),
        forward_y,
        "ky,czyx->czkx",
        readout,
    )
    spectrum = jnp.where(column_mask, spectrum, nothing)
    spectrum = transform(spectrum, inverse_y, "ky,czyx->czkx", readout)
    coil_block = lax.all_to_all(spectrum, "pencil", split_axis=2, concat_axis=1, tiled=True)
    coil_block = transform(coil_block, inverse_z, "kz,czyx->ckyx", readout)
    returned = jnp.dot(coil_block, inverse_x, preferred_element_type=jnp.float32).astype(
        jnp.bfloat16
    )
    partial_sum = jnp.sum(complex_product(coil_maps, returned, readout, True), axis=0)
    return lax.psum_scatter(
        partial_sum.astype(jnp.bfloat16), "coil", scatter_dimension=0, tiled=True
    ).astype(jnp.float32)


MESH = pl.DeviceIdType.MESH


def fixed_tables(length, direction):
    indices = np.arange(length, dtype=np.int32)
    phases = indices[:, None] * indices[None, :] % length
    angles = phases.astype(np.float32) * np.float32(2.0 * math.pi / length)
    factor = np.float32(1.0 / math.sqrt(length))
    cosine, sine_part = np.cos(angles) * factor, np.float32(direction) * np.sin(angles) * factor
    return cosine.astype(jnp.bfloat16), sine_part.astype(jnp.bfloat16)


def rotation(cosine, sine_part, rows):
    if rows:
        return np.block([[cosine, sine_part], [-sine_part, cosine]])
    return np.block([[cosine, -sine_part], [sine_part, cosine]])


def plan_tables(slices, lines, readout, group):
    quarter, half_y, half_z = readout // 4, lines // 2, slices // 2

    def wide(part):
        return np.kron(part.astype(np.float32), np.eye(group, dtype=np.float32)).astype(part.dtype)

    cx, sx = fixed_tables(readout, -1.0)
    x_fwd = np.stack([rotation(cx[:quarter, r::4], sx[:quarter, r::4], True) for r in range(4)])
    cx, sx = fixed_tables(readout, 1.0)
    x_inv = np.stack([rotation(cx[r::4, :quarter], sx[r::4, :quarter], True) for r in range(4)])
    cy, sy = fixed_tables(lines, -1.0)
    y_fwd = np.stack([rotation(cy[p::2, :half_y], sy[p::2, :half_y], False) for p in range(2)])
    cy, sy = fixed_tables(lines, 1.0)
    y_inv = np.stack([rotation(cy[:half_y, p::2], sy[:half_y, p::2], False) for p in range(2)])
    cz, sz = fixed_tables(slices, -1.0)
    z_fwd = [rotation(wide(cz[p::2, :half_z]), wide(sz[p::2, :half_z]), False) for p in range(2)]
    cz, sz = fixed_tables(slices, 1.0)
    z_inv = [rotation(wide(cz[:half_z, p::2]), wide(sz[:half_z, p::2]), False) for p in range(2)]
    return [jnp.asarray(t) for t in (x_fwd, x_inv, y_fwd, y_inv, np.stack(z_fwd), np.stack(z_inv))]


def mm(left, right):
    return jnp.dot(left, right, preferred_element_type=jnp.float32)


def forward_body(map_part, image_part, x_fwd, y_fwd):
    lines = map_part.shape[0]
    readout = map_part.shape[1] // 2
    quarter, half = readout // 4, lines // 2
    left = map_part.astype(jnp.float32)
    right = image_part.astype(jnp.float32)
    re, im = [], []
    for q in range(4):
        a, b = q * quarter, (q + 1) * quarter
        lr, li = left[:, a:b], left[:, readout + a : readout + b]
        rr, ri = right[:, a:b], right[:, readout + a : readout + b]
        re.append(lr * rr - li * ri)
        im.append(lr * ri + li * rr)
    sum_re, sum_im = re[0] + re[2], im[0] + im[2]
    dif_re, dif_im = re[0] - re[2], im[0] - im[2]
    odd_re, odd_im = re[1] + re[3], im[1] + im[3]
    tur_re, tur_im = re[1] - re[3], im[1] - im[3]
    mixed = [
        (sum_re + odd_re, sum_im + odd_im),
        (dif_re + tur_im, dif_im - tur_re),
        (sum_re - odd_re, sum_im - odd_im),
        (dif_re - tur_im, dif_im + tur_re),
    ]
    even, odd = [], []
    for r in range(4):
        v = mm(jnp.concatenate(mixed[r], axis=1).astype(jnp.bfloat16), x_fwd[r])
        e = (v[:half] + v[half:]).astype(jnp.bfloat16)
        o = (v[:half] - v[half:]).astype(jnp.bfloat16)
        even.append(jnp.concatenate([e[:, :quarter], e[:, quarter:]], axis=0))
        odd.append(jnp.concatenate([o[:, :quarter], o[:, quarter:]], axis=0))
    even = mm(y_fwd[0], jnp.concatenate(even, axis=1)).astype(jnp.bfloat16)
    odd = mm(y_fwd[1], jnp.concatenate(odd, axis=1)).astype(jnp.bfloat16)
    return even, odd


def slab_body(block, mask_block, z_fwd, z_inv):
    slices, group, width = block.shape
    half, readout = slices // 2, width // 2
    flat = half * group
    low = block[:half].astype(jnp.float32)
    high = block[half:].astype(jnp.float32)
    parts = [low + high, low - high]
    back = []
    for p in range(2):
        u = parts[p].astype(jnp.bfloat16).reshape(flat, width)
        u = jnp.concatenate([u[:, :readout], u[:, readout:]], axis=0)
        k = mm(z_fwd[p], u)
        m = mask_block[p].reshape(flat, readout // 4).astype(jnp.float32)
        m = jnp.concatenate([m] * 4, axis=1)
        k = jnp.concatenate([k[:flat] * m, k[flat:] * m], axis=0).astype(jnp.bfloat16)
        back.append(mm(z_inv[p], k))

    def place(t):
        t = t.astype(jnp.bfloat16)
        return jnp.concatenate([t[:flat], t[flat:]], axis=1).reshape(half, group, width)

    return place(back[0] + back[1]), place(back[0] - back[1])


def backward_body(block, map_part, x_inv, y_inv):
    lines = block.shape[0]
    readout = block.shape[1] // 2
    quarter, half = readout // 4, lines // 2
    sides = []
    for p in range(2):
        part = block[p * half : (p + 1) * half]
        sides.append(mm(y_inv[p], jnp.concatenate([part[:, :readout], part[:, readout:]], axis=0)))
    lows = (sides[0] + sides[1]).astype(jnp.bfloat16)
    highs = (sides[0] - sides[1]).astype(jnp.bfloat16)
    t_re, t_im = [], []
    for r in range(4):
        a, b = r * quarter, (r + 1) * quarter
        rows = jnp.concatenate(
            [
                jnp.concatenate([lows[:half, a:b], lows[half:, a:b]], axis=1),
                jnp.concatenate([highs[:half, a:b], highs[half:, a:b]], axis=1),
            ],
            axis=0,
        )
        t = mm(rows, x_inv[r])
        t_re.append(t[:, :quarter])
        t_im.append(t[:, quarter:])
    sr, si = t_re[0] + t_re[2], t_im[0] + t_im[2]
    dr, di = t_re[0] - t_re[2], t_im[0] - t_im[2]
    er, ei = t_re[1] + t_re[3], t_im[1] + t_im[3]
    fr, fi = t_re[1] - t_re[3], t_im[1] - t_im[3]
    image = [(sr + er, si + ei), (dr - fi, di + fr), (sr - er, si - ei), (dr + fi, di - fr)]
    maps = map_part.astype(jnp.float32)
    out_re, out_im = [], []
    for q in range(4):
        a, b = q * quarter, (q + 1) * quarter
        mr, mi = maps[:, a:b], maps[:, readout + a : readout + b]
        xr, xi = image[q]
        out_re.append(mr * xr + mi * xi)
        out_im.append(mr * xi - mi * xr)
    return jnp.concatenate(out_re + out_im, axis=1)


def image_rows(image_ref):
    chips = image_ref.shape[2]
    return jnp.concatenate([image_ref[i % 2, 0, i // 2] for i in range(2 * chips)], axis=0)


def exchange_call(coil_maps, object_image, mask, x_fwd, y_fwd, z_fwd, z_inv, group):
    pencils, columns = lax.axis_size("pencil"), lax.axis_size("coil")
    coils, slices, rows, width = coil_maps.shape
    per, chips, share = coils // pencils, pencils // 2, slices // columns
    lines, readout = rows * pencils, width // 2
    half_y, half_z = lines // 2, slices // 2
    shifts = sorted(range(1, pencils), key=lambda s: abs(s - pencils // 2))

    def kernel(
        map_ref, image_ref, mask_ref, xf_ref, yf_ref, zf_ref, zi_ref,
        out_ref, full_ref, mid_ref, vol_ref,
        own_sem, map_send, map_recv, im_send, im_recv, col_send, col_recv, core_send, core_recv,
    ):
        me, column = lax.axis_index("pencil"), lax.axis_index("coil")
        chip, core = me // 2, me % 2

        barrier = pltpu.get_barrier_semaphore()
        for s in range(1, pencils):
            pl.semaphore_signal(
                barrier, device_id=(column, lax.rem(me + s, pencils)), device_id_type=MESH
            )
        for s in range(1, columns):
            pl.semaphore_signal(
                barrier, device_id=(lax.rem(column + s, columns), me), device_id_type=MESH
            )
        pl.semaphore_wait(barrier, pencils + columns - 2)

        quarter = pl.ds(column * share, share)
        own_image = pltpu.make_async_copy(
            image_ref.at[quarter], full_ref.at[core, quarter, chip], own_sem.at[per]
        )
        own = [
            pltpu.make_async_copy(
                map_ref.at[me * per + j], out_ref.at[j, :, pl.ds(me * rows, rows)], own_sem.at[j]
            )
            for j in range(per)
        ]
        along = [
            pltpu.make_async_remote_copy(
                src_ref=image_ref.at[quarter],
                dst_ref=full_ref.at[core, quarter, chip],
                send_sem=im_send.at[s - 1],
                recv_sem=im_recv.at[s - 1],
                device_id=(column, lax.rem(me + 2 * s, pencils)),
                device_id_type=MESH,
            )
            for s in range(1, chips)
        ]
        moves = [
            [
                pltpu.make_async_remote_copy(
                    src_ref=map_ref.at[lax.rem(me + s, pencils) * per + j],
                    dst_ref=out_ref.at[j, :, pl.ds(me * rows, rows)],
                    send_sem=map_send.at[j, i],
                    recv_sem=map_recv.at[j, i],
                    device_id=(column, lax.rem(me + s, pencils)),
                    device_id_type=MESH,
                )
                for i, s in enumerate(shifts)
            ]
            for j in range(per)
        ]
        for copy in along + moves[0] + [own_image] + own:
            copy.start()
        own_image.wait()
        for copy in along:
            copy.wait()
        across = [
            pltpu.make_async_remote_copy(
                src_ref=full_ref.at[core, quarter],
                dst_ref=full_ref.at[core, quarter],
                send_sem=col_send.at[s - 1],
                recv_sem=col_recv.at[s - 1],
                device_id=(lax.rem(column + s, columns), me),
                device_id_type=MESH,
            )
            for s in range(1, columns)
        ]
        for copy in across:
            copy.start()
        for copy in across:
            copy.wait()
        pair = pltpu.make_async_remote_copy(
            src_ref=full_ref.at[core],
            dst_ref=full_ref.at[core],
            send_sem=core_send,
            recv_sem=core_recv,
            device_id=(column, me + 1 - 2 * core),
            device_id_type=MESH,
        )
        pair.start()
        pair.wait()

        def forward(map_block, image_block, o_ref):
            even, odd = forward_body(map_block[0], image_rows(image_block), xf_ref, yf_ref)
            o_ref[0, :half_y, :readout] = even[:half_y]
            o_ref[0, :half_y, readout:] = even[half_y:]
            o_ref[0, half_y:, :readout] = odd[:half_y]
            o_ref[0, half_y:, readout:] = odd[half_y:]

        def slab(block, mask_block, o_ref):
            low, high = slab_body(block[...], mask_block[...], zf_ref, zi_ref)
            o_ref[:half_z] = low
            o_ref[half_z:] = high

        plane = pl.BlockSpec((1, lines, width), lambda z: (z, 0, 0))
        image_spec = pl.BlockSpec((2, 1, chips, rows, width), lambda z: (0, z, 0, 0, 0))
        slab_spec = pl.BlockSpec((slices, group, width), lambda y: (0, y, 0))
        mask_spec = pl.BlockSpec((2, half_z, group, readout // 4), lambda y: (0, 0, y, 0))
        for j in range(per):
            for i in range(len(shifts)):
                moves[j][i].wait_send()
                if j + 1 < per:
                    moves[j + 1][i].start()
            for copy in moves[j]:
                copy.wait_recv()
            own[j].wait()
            pltpu.emit_pipeline(
                forward, grid=(slices,), in_specs=[plane, image_spec], out_specs=[plane]
            )(out_ref.at[j], full_ref, mid_ref.at[j])
            pltpu.emit_pipeline(
                slab, grid=(lines // group,), in_specs=[slab_spec, mask_spec], out_specs=[slab_spec]
            )(mid_ref.at[j], mask_ref, vol_ref.at[j])

    dma = pltpu.SemaphoreType.DMA
    anywhere = pl.BlockSpec(memory_space=pl.ANY)
    vmem = pl.BlockSpec(memory_space=pltpu.VMEM)
    whole = jax.ShapeDtypeStruct((per, slices, lines, width), jnp.bfloat16)
    return pl.pallas_call(
        kernel,
        out_shape=[
            whole,
            jax.ShapeDtypeStruct((2, slices, chips, rows, width), jnp.bfloat16),
            whole,
            whole,
        ],
        in_specs=[anywhere, anywhere, anywhere, vmem, vmem, vmem, vmem],
        out_specs=[anywhere] * 4,
        scratch_shapes=[
            dma((per + 1,)),
            dma((per, pencils - 1)),
            dma((per, pencils - 1)),
            dma((chips - 1,)),
            dma((chips - 1,)),
            dma((columns - 1,)),
            dma((columns - 1,)),
            dma,
            dma,
        ],
        compiler_params=pltpu.CompilerParams(
            collective_id=0, has_side_effects=True, vmem_limit_bytes=56 << 20
        ),
        name="exchange_forward",
    )(coil_maps, object_image, mask, x_fwd, y_fwd, z_fwd, z_inv)


def combine_call(volume, maps, x_inv, y_inv):
    pencils, columns = lax.axis_size("pencil"), lax.axis_size("coil")
    per, slices, lines, width = volume.shape
    rows, chips, share = lines // pencils, pencils // 2, slices // columns
    volume = volume.reshape(per, columns, share, lines, width)
    maps = maps.reshape(per, columns, share, lines, width)

    def kernel(
        vol_ref, map_ref, xi_ref, yi_ref, part_ref, out_ref,
        mine, from_core, from_column, column_sum, from_chip,
        own_sem, core_send, core_recv, col_send, col_recv, chip_send, chip_recv,
    ):
        me, column = lax.axis_index("pencil"), lax.axis_index("coil")
        chip, core = me // 2, me % 2

        barrier = pltpu.get_barrier_semaphore()
        pl.semaphore_signal(barrier, device_id=(column, me + 1 - 2 * core), device_id_type=MESH)
        for s in range(1, columns):
            pl.semaphore_signal(
                barrier, device_id=(lax.rem(column + s, columns), me), device_id_type=MESH
            )
        for s in range(1, chips):
            pl.semaphore_signal(
                barrier, device_id=(column, lax.rem(me + 2 * s, pencils)), device_id_type=MESH
            )
        pl.semaphore_wait(barrier, columns + chips - 1)

        def own_copy(k):
            return pltpu.make_async_copy(part_ref.at[k, core], mine.at[k], own_sem.at[k])

        def core_copy(k):
            return pltpu.make_async_remote_copy(
                src_ref=part_ref.at[k, 1 - core],
                dst_ref=from_core.at[k],
                send_sem=core_send.at[k],
                recv_sem=core_recv.at[k],
                device_id=(column, me + 1 - 2 * core),
                device_id_type=MESH,
            )

        def column_copy(k, s):
            target = lax.rem(column + s, columns)
            return pltpu.make_async_remote_copy(
                src_ref=mine.at[k, target],
                dst_ref=from_column.at[k, s - 1],
                send_sem=col_send.at[k, s - 1],
                recv_sem=col_recv.at[k, s - 1],
                device_id=(target, me),
                device_id_type=MESH,
            )

        def chip_copy(k, s):
            target = lax.rem(chip + s, chips)
            return pltpu.make_async_remote_copy(
                src_ref=column_sum.at[k, target],
                dst_ref=from_chip.at[k, s - 1],
                send_sem=chip_send.at[k, s - 1],
                recv_sem=chip_recv.at[k, s - 1],
                device_id=(column, 2 * target + core),
                device_id_type=MESH,
            )

        def backward(block, map_block, o_ref):
            total = backward_body(block[0, 0], map_block[0, 0], xi_ref, yi_ref)
            for j in range(1, per):
                total += backward_body(block[j, 0], map_block[j, 0], xi_ref, yi_ref)
            total = total.astype(o_ref.dtype)
            for i in range(pencils):
                o_ref[i % 2, 0, i // 2] = total[i * rows : (i + 1) * rows]

        plane = pl.BlockSpec((per, 1, lines, width), lambda c: (0, c, 0, 0))
        part_spec = pl.BlockSpec((2, 1, chips, rows, width), lambda c: (0, c, 0, 0, 0))

        def step(t, carry):
            @pl.when(t < share)
            def _():
                pltpu.emit_pipeline(
                    backward, grid=(columns,), in_specs=[plane, plane], out_specs=[part_spec]
                )(vol_ref.at[:, :, t], map_ref.at[:, :, t], part_ref.at[t])
                core_copy(t).start()
                own_copy(t).start()

            @pl.when((t >= 1) & (t < share + 1))
            def _():
                k = t - 1
                own_copy(k).wait()
                core_copy(k).wait_recv()
                for c in range(columns):
                    for z in range(chips):
                        mine[k, c, z] = (
                            mine[k, c, z].astype(jnp.float32)
                            + from_core[k, c, z].astype(jnp.float32)
                        ).astype(jnp.bfloat16)
                for s in range(1, columns):
                    column_copy(k, s).start()

            @pl.when((t >= 2) & (t < share + 2))
            def _():
                k = t - 2
                for s in range(1, columns):
                    column_copy(k, s).wait_recv()
                for z in range(chips):
                    total = mine[k, column, z].astype(jnp.float32)
                    for s in range(1, columns):
                        total += from_column[k, s - 1, z].astype(jnp.float32)
                    column_sum[k, z] = total.astype(jnp.bfloat16)
                for s in range(1, chips):
                    chip_copy(k, s).start()

            @pl.when(t >= 3)
            def _():
                k = t - 3
                for s in range(1, chips):
                    chip_copy(k, s).wait_recv()
                total = column_sum[k, chip].astype(jnp.float32)
                for s in range(1, chips):
                    total += from_chip[k, s - 1].astype(jnp.float32)
                out_ref[k] = total

            return carry

        lax.fori_loop(0, share + 3, step, 0)

        def finish(k, carry):
            core_copy(k).wait_send()
            for s in range(1, columns):
                column_copy(k, s).wait_send()
            for s in range(1, chips):
                chip_copy(k, s).wait_send()
            return carry

        lax.fori_loop(0, share, finish, 0)

    dma = pltpu.SemaphoreType.DMA
    anywhere = pl.BlockSpec(memory_space=pl.ANY)
    vmem = pl.BlockSpec(memory_space=pltpu.VMEM)
    block = (chips, rows, width)
    return pl.pallas_call(
        kernel,
        out_shape=[
            jax.ShapeDtypeStruct((share, 2, columns) + block, jnp.bfloat16),
            jax.ShapeDtypeStruct((share, rows, width), jnp.float32),
        ],
        in_specs=[anywhere, anywhere, vmem, vmem],
        out_specs=[anywhere, vmem],
        scratch_shapes=[
            pltpu.VMEM((share, columns) + block, jnp.bfloat16),
            pltpu.VMEM((share, columns) + block, jnp.bfloat16),
            pltpu.VMEM((share, columns - 1) + block, jnp.bfloat16),
            pltpu.VMEM((share,) + block, jnp.bfloat16),
            pltpu.VMEM((share, chips - 1, rows, width), jnp.bfloat16),
            dma((share,)),
            dma((share,)),
            dma((share,)),
            dma((share, columns - 1)),
            dma((share, columns - 1)),
            dma((share, chips - 1)),
            dma((share, chips - 1)),
        ],
        compiler_params=pltpu.CompilerParams(
            collective_id=1, has_side_effects=True, vmem_limit_bytes=60 << 20
        ),
        name="backward_combine",
    )(volume, maps, x_inv, y_inv)[1]


def plan_mask(sample_mask, readout):
    slices, lines, segments = sample_mask.shape
    run = readout // segments // 4
    flags = sample_mask.reshape(slices // 2, 2, lines // 2, 2, segments).transpose(1, 0, 3, 2, 4)
    flags = (flags > 0).astype(jnp.bfloat16).reshape(2, slices // 2, lines, segments)
    return jnp.repeat(flags, run, axis=3)


def whole_coils(object_image, coil_maps, sample_mask):
    readout = object_image.shape[2] // 2
    slices = object_image.shape[0]
    lines = object_image.shape[1] * lax.axis_size("pencil")
    group = 16
    x_fwd, x_inv, y_fwd, y_inv, z_fwd, z_inv = plan_tables(slices, lines, readout, group)
    mask = plan_mask(sample_mask, readout)
    maps, _, _, volume = exchange_call(
        coil_maps, object_image, mask, x_fwd, y_fwd, z_fwd, z_inv, group
    )
    return combine_call(volume, maps, x_inv, y_inv)


def solution(mesh):
    placed = (P(None, "pencil", None), P("coil", None, "pencil", None), P())

    def on_device(object_image, coil_maps, sample_mask):
        whole = coil_maps.shape[0] % lax.axis_size("pencil") == 0
        return (whole_coils if whole else split_lines)(object_image, coil_maps, sample_mask)

    return jax.shard_map(
        on_device, mesh=mesh, in_specs=placed, out_specs=P("coil", "pencil", None), check_vma=False
    )
```

```python
import math

import numpy as np

import jax
import jax.numpy as jnp
from jax import lax
from jax.experimental import pallas as pl
from jax.experimental.pallas import tpu as pltpu
from jax.sharding import PartitionSpec as P


def dft_tables(length, direction):
    indices = jnp.arange(length, dtype=jnp.int32)
    phases = indices[:, None] * indices[None, :] % length
    angles = phases.astype(jnp.float32) * (2.0 * math.pi / length)
    factor = 1.0 / math.sqrt(length)
    cosine = (jnp.cos(angles) * factor).astype(jnp.bfloat16)
    sine_part = (direction * jnp.sin(angles) * factor).astype(jnp.bfloat16)
    return (cosine, sine_part)


def readout_table(length, direction):
    cosine, sine_part = dft_tables(length, direction)
    upper = jnp.concatenate([cosine, sine_part], axis=1)
    lower = jnp.concatenate([-sine_part, cosine], axis=1)
    return jnp.concatenate([upper, lower], axis=0)


def complex_product(left_side, right_side, readout, conjugate):
    left_full = left_side.astype(jnp.float32)
    right_full = right_side.astype(jnp.float32)
    left_real = left_full[..., :readout]
    left_imag = left_full[..., readout:]
    if conjugate:
        left_imag = -left_imag
    right_real = right_full[..., :readout]
    right_imag = right_full[..., readout:]
    real_part = left_real * right_real - left_imag * right_imag
    imag_part = left_real * right_imag + left_imag * right_real
    return jnp.concatenate([real_part, imag_part], axis=-1)


def transform(volume, tables, formula, readout):
    cosine, sine_part = tables
    direct = jnp.einsum(formula, cosine, volume, preferred_element_type=jnp.float32)
    crossed = jnp.einsum(formula, sine_part, volume, preferred_element_type=jnp.float32)
    turned = jnp.concatenate([-crossed[..., readout:], crossed[..., :readout]], axis=-1)
    return (direct + turned).astype(jnp.bfloat16)


def widen(mask_part, segment):
    flags = jnp.repeat(mask_part, segment, axis=2) > 0
    return jnp.concatenate([flags, flags], axis=2)


def split_lines(object_image, coil_maps, sample_mask):
    readout = object_image.shape[2] // 2
    slices = object_image.shape[0]
    row_count = object_image.shape[1]
    pencils = lax.axis_size("pencil")
    depth = slices // pencils
    lines = row_count * pencils
    segment = readout // sample_mask.shape[2]
    position = lax.axis_index("pencil")
    forward_x = readout_table(readout, -1.0)
    inverse_x = readout_table(readout, 1.0)
    forward_z = dft_tables(slices, -1.0)
    inverse_z = dft_tables(slices, 1.0)
    forward_y = dft_tables(lines, -1.0)
    inverse_y = dft_tables(lines, 1.0)
    column_mask = widen(lax.dynamic_slice_in_dim(sample_mask, position * depth, depth, 0), segment)
    nothing = jnp.zeros((), jnp.bfloat16)
    coil_image = complex_product(coil_maps, object_image[None], readout, False).astype(jnp.bfloat16)
    volume = jnp.dot(coil_image, forward_x, preferred_element_type=jnp.float32).astype(jnp.bfloat16)
    volume = transform(volume, forward_z, "kz,czyx->ckyx", readout)
    spectrum = transform(
        lax.all_to_all(volume, "pencil", split_axis=1, concat_axis=2, tiled=True),
        forward_y,
        "ky,czyx->czkx",
        readout,
    )
    spectrum = jnp.where(column_mask, spectrum, nothing)
    spectrum = transform(spectrum, inverse_y, "ky,czyx->czkx", readout)
    coil_block = lax.all_to_all(spectrum, "pencil", split_axis=2, concat_axis=1, tiled=True)
    coil_block = transform(coil_block, inverse_z, "kz,czyx->ckyx", readout)
    returned = jnp.dot(coil_block, inverse_x, preferred_element_type=jnp.float32).astype(
        jnp.bfloat16
    )
    partial_sum = jnp.sum(complex_product(coil_maps, returned, readout, True), axis=0)
    return lax.psum_scatter(
        partial_sum.astype(jnp.bfloat16), "coil", scatter_dimension=0, tiled=True
    ).astype(jnp.float32)


MESH = pl.DeviceIdType.MESH


def fixed_tables(length, direction):
    indices = np.arange(length, dtype=np.int32)
    phases = indices[:, None] * indices[None, :] % length
    angles = phases.astype(np.float32) * np.float32(2.0 * math.pi / length)
    factor = np.float32(1.0 / math.sqrt(length))
    cosine, sine_part = np.cos(angles) * factor, np.float32(direction) * np.sin(angles) * factor
    return cosine.astype(jnp.bfloat16), sine_part.astype(jnp.bfloat16)


def rotation(cosine, sine_part, rows):
    if rows:
        return np.block([[cosine, sine_part], [-sine_part, cosine]])
    return np.block([[cosine, -sine_part], [sine_part, cosine]])


def plan_tables(slices, lines, readout, group):
    quarter, half_y, half_z = readout // 4, lines // 2, slices // 2

    def wide(part):
        return np.kron(part.astype(np.float32), np.eye(group, dtype=np.float32)).astype(part.dtype)

    cx, sx = fixed_tables(readout, -1.0)
    x_fwd = np.stack([rotation(cx[:quarter, r::4], sx[:quarter, r::4], True) for r in range(4)])
    cx, sx = fixed_tables(readout, 1.0)
    x_inv = np.stack([rotation(cx[r::4, :quarter], sx[r::4, :quarter], True) for r in range(4)])
    cy, sy = fixed_tables(lines, -1.0)
    y_fwd = np.stack([rotation(cy[p::2, :half_y], sy[p::2, :half_y], False) for p in range(2)])
    cy, sy = fixed_tables(lines, 1.0)
    y_inv = np.stack([rotation(cy[:half_y, p::2], sy[:half_y, p::2], False) for p in range(2)])
    cz, sz = fixed_tables(slices, -1.0)
    z_fwd = [rotation(wide(cz[p::2, :half_z]), wide(sz[p::2, :half_z]), False) for p in range(2)]
    cz, sz = fixed_tables(slices, 1.0)
    z_inv = [rotation(wide(cz[:half_z, p::2]), wide(sz[:half_z, p::2]), False) for p in range(2)]
    return [jnp.asarray(t) for t in (x_fwd, x_inv, y_fwd, y_inv, np.stack(z_fwd), np.stack(z_inv))]


def mm(left, right):
    return jnp.dot(left, right, preferred_element_type=jnp.float32)


def forward_body(map_part, image_part, x_fwd, y_fwd):
    lines = map_part.shape[0]
    readout = map_part.shape[1] // 2
    quarter, half = readout // 4, lines // 2
    left = map_part.astype(jnp.float32)
    right = image_part.astype(jnp.float32)
    re, im = [], []
    for q in range(4):
        a, b = q * quarter, (q + 1) * quarter
        lr, li = left[:, a:b], left[:, readout + a : readout + b]
        rr, ri = right[:, a:b], right[:, readout + a : readout + b]
        re.append(lr * rr - li * ri)
        im.append(lr * ri + li * rr)
    sum_re, sum_im = re[0] + re[2], im[0] + im[2]
    dif_re, dif_im = re[0] - re[2], im[0] - im[2]
    odd_re, odd_im = re[1] + re[3], im[1] + im[3]
    tur_re, tur_im = re[1] - re[3], im[1] - im[3]
    mixed = [
        (sum_re + odd_re, sum_im + odd_im),
        (dif_re + tur_im, dif_im - tur_re),
        (sum_re - odd_re, sum_im - odd_im),
        (dif_re - tur_im, dif_im + tur_re),
    ]
    even, odd = [], []
    for r in range(4):
        v = mm(jnp.concatenate(mixed[r], axis=1).astype(jnp.bfloat16), x_fwd[r])
        e = (v[:half] + v[half:]).astype(jnp.bfloat16)
        o = (v[:half] - v[half:]).astype(jnp.bfloat16)
        even.append(jnp.concatenate([e[:, :quarter], e[:, quarter:]], axis=0))
        odd.append(jnp.concatenate([o[:, :quarter], o[:, quarter:]], axis=0))
    even = mm(y_fwd[0], jnp.concatenate(even, axis=1)).astype(jnp.bfloat16)
    odd = mm(y_fwd[1], jnp.concatenate(odd, axis=1)).astype(jnp.bfloat16)
    return even, odd


def slab_body(block, mask_block, z_fwd, z_inv):
    slices, group, width = block.shape
    half, readout = slices // 2, width // 2
    flat = half * group
    low = block[:half].astype(jnp.float32)
    high = block[half:].astype(jnp.float32)
    parts = [low + high, low - high]
    back = []
    for p in range(2):
        u = parts[p].astype(jnp.bfloat16).reshape(flat, width)
        u = jnp.concatenate([u[:, :readout], u[:, readout:]], axis=0)
        k = mm(z_fwd[p], u)
        m = mask_block[p].reshape(flat, readout // 4).astype(jnp.float32)
        m = jnp.concatenate([m] * 4, axis=1)
        k = jnp.concatenate([k[:flat] * m, k[flat:] * m], axis=0).astype(jnp.bfloat16)
        back.append(mm(z_inv[p], k))

    def place(t):
        t = t.astype(jnp.bfloat16)
        return jnp.concatenate([t[:flat], t[flat:]], axis=1).reshape(half, group, width)

    return place(back[0] + back[1]), place(back[0] - back[1])


def backward_body(block, map_part, x_inv, y_inv):
    lines = block.shape[0]
    readout = block.shape[1] // 2
    quarter, half = readout // 4, lines // 2
    sides = []
    for p in range(2):
        part = block[p * half : (p + 1) * half]
        sides.append(mm(y_inv[p], jnp.concatenate([part[:, :readout], part[:, readout:]], axis=0)))
    lows = (sides[0] + sides[1]).astype(jnp.bfloat16)
    highs = (sides[0] - sides[1]).astype(jnp.bfloat16)
    t_re, t_im = [], []
    for r in range(4):
        a, b = r * quarter, (r + 1) * quarter
        rows = jnp.concatenate(
            [
                jnp.concatenate([lows[:half, a:b], lows[half:, a:b]], axis=1),
                jnp.concatenate([highs[:half, a:b], highs[half:, a:b]], axis=1),
            ],
            axis=0,
        )
        t = mm(rows, x_inv[r])
        t_re.append(t[:, :quarter])
        t_im.append(t[:, quarter:])
    sr, si = t_re[0] + t_re[2], t_im[0] + t_im[2]
    dr, di = t_re[0] - t_re[2], t_im[0] - t_im[2]
    er, ei = t_re[1] + t_re[3], t_im[1] + t_im[3]
    fr, fi = t_re[1] - t_re[3], t_im[1] - t_im[3]
    image = [(sr + er, si + ei), (dr - fi, di + fr), (sr - er, si - ei), (dr + fi, di - fr)]
    maps = map_part.astype(jnp.float32)
    out_re, out_im = [], []
    for q in range(4):
        a, b = q * quarter, (q + 1) * quarter
        mr, mi = maps[:, a:b], maps[:, readout + a : readout + b]
        xr, xi = image[q]
        out_re.append(mr * xr + mi * xi)
        out_im.append(mr * xi - mi * xr)
    return jnp.concatenate(out_re + out_im, axis=1)


def image_rows(image_ref):
    chips = image_ref.shape[2]
    return jnp.concatenate([image_ref[i % 2, 0, i // 2] for i in range(2 * chips)], axis=0)


def flip(value, bits):
    bit = 1
    while bit <= bits:
        if bits & bit:
            value = value + bit - 2 * bit * ((value // bit) % 2)
        bit *= 2
    return value


def exchange_call(coil_maps, object_image, mask, tables, group, pieces):
    pencils, columns = lax.axis_size("pencil"), lax.axis_size("coil")
    coils, slices, rows, width = coil_maps.shape
    per, chips, share = coils // pencils, pencils // 2, slices // columns
    lines, readout = rows * pencils, width // 2
    half_y, half_z = lines // 2, slices // 2
    shifts = sorted(range(1, pencils), key=lambda s: abs(s - pencils // 2))
    last, run = per - 1, slices // pieces

    def kernel(
        map_ref, image_ref, mask_ref, xf_ref, xi_ref, yf_ref, yi_ref, zf_ref, zi_ref,
        out_ref, full_ref, mid_ref, vol_ref, part_ref,
        own_sem, map_send, map_recv, end_send, end_recv, im_send, im_recv, col_send, col_recv, core_send, core_recv,
    ):
        me, column = lax.axis_index("pencil"), lax.axis_index("coil")
        chip, core = me // 2, me % 2

        barrier = pltpu.get_barrier_semaphore()
        for s in range(1, pencils):
            pl.semaphore_signal(
                barrier, device_id=(column, lax.rem(me + s, pencils)), device_id_type=MESH
            )
        for s in range(1, columns):
            pl.semaphore_signal(
                barrier, device_id=(lax.rem(column + s, columns), me), device_id_type=MESH
            )
        pl.semaphore_wait(barrier, pencils + columns - 2)

        quarter = pl.ds(column * share, share)
        own_image = pltpu.make_async_copy(
            image_ref.at[quarter], full_ref.at[core, quarter, chip], own_sem.at[per]
        )
        own = [
            pltpu.make_async_copy(
                map_ref.at[me * per + j], out_ref.at[j, :, pl.ds(me * rows, rows)], own_sem.at[j]
            )
            for j in range(per)
        ]
        moves = [
            [
                pltpu.make_async_remote_copy(
                    src_ref=map_ref.at[lax.rem(me + s, pencils) * per + j],
                    dst_ref=out_ref.at[j, :, pl.ds(me * rows, rows)],
                    send_sem=map_send.at[j, i],
                    recv_sem=map_recv.at[j, i],
                    device_id=(column, lax.rem(me + s, pencils)),
                    device_id_type=MESH,
                )
                for i, s in enumerate(shifts)
            ]
            for j in range(last)
        ]
        ends = [
            [
                pltpu.make_async_remote_copy(
                    src_ref=map_ref.at[
                        lax.rem(me + s, pencils) * per + last, pl.ds(g * run, run)
                    ],
                    dst_ref=out_ref.at[last, pl.ds(g * run, run), pl.ds(me * rows, rows)],
                    send_sem=end_send.at[g, i],
                    recv_sem=end_recv.at[g, i],
                    device_id=(column, lax.rem(me + s, pencils)),
                    device_id_type=MESH,
                )
                for i, s in enumerate(shifts)
            ]
            for g in range(pieces)
        ]

        def along(d, n, h):
            block = full_ref.at[core, quarter, flip(chip, h)]
            return pltpu.make_async_remote_copy(
                src_ref=block,
                dst_ref=block,
                send_sem=im_send.at[n],
                recv_sem=im_recv.at[n],
                device_id=(column, 2 * flip(chip, d) + core),
                device_id_type=MESH,
            )

        own_image.start()
        own_image.wait()
        held, d, first = [0], chips // 2, True
        while d >= 1:
            copies = [along(d, len(held) - 1 + n, h) for n, h in enumerate(held)]
            for copy in copies:
                copy.start()
            if first:
                for copy in moves[0] + own:
                    copy.start()
            for copy in copies:
                copy.wait()
            held, d, first = held + [h ^ d for h in held], d // 2, False
        across = [
            pltpu.make_async_remote_copy(
                src_ref=full_ref.at[core, quarter],
                dst_ref=full_ref.at[core, quarter],
                send_sem=col_send.at[s - 1],
                recv_sem=col_recv.at[s - 1],
                device_id=(lax.rem(column + s, columns), me),
                device_id_type=MESH,
            )
            for s in range(1, columns)
        ]
        for copy in across:
            copy.start()
        for copy in across:
            copy.wait()
        pair = pltpu.make_async_remote_copy(
            src_ref=full_ref.at[core],
            dst_ref=full_ref.at[core],
            send_sem=core_send,
            recv_sem=core_recv,
            device_id=(column, me + 1 - 2 * core),
            device_id_type=MESH,
        )
        pair.start()
        pair.wait()

        def forward(map_block, image_block, o_ref):
            even, odd = forward_body(map_block[0], image_rows(image_block), xf_ref, yf_ref)
            o_ref[0, :half_y, :readout] = even[:half_y]
            o_ref[0, :half_y, readout:] = even[half_y:]
            o_ref[0, half_y:, :readout] = odd[:half_y]
            o_ref[0, half_y:, readout:] = odd[half_y:]

        def slab(block, mask_block, o_ref):
            low, high = slab_body(block[...], mask_block[...], zf_ref, zi_ref)
            o_ref[:half_z] = low
            o_ref[half_z:] = high

        plane = pl.BlockSpec((1, lines, width), lambda z: (z, 0, 0))
        image_spec = pl.BlockSpec((2, 1, chips, rows, width), lambda z: (0, z, 0, 0, 0))
        slab_spec = pl.BlockSpec((slices, group, width), lambda y: (0, y, 0))
        mask_spec = pl.BlockSpec((2, half_z, group, readout // 4), lambda y: (0, 0, y, 0))
        part_spec = pl.BlockSpec(
            (1, 2, 1, chips, rows, width), lambda k, c: (k, 0, c, 0, 0, 0)
        )
        strided = pl.BlockSpec((1, lines, width), lambda k, c: (c * share + k, 0, 0))

        def backward(block, map_block, o_ref):
            total = backward_body(block[0], map_block[0], xi_ref, yi_ref).astype(o_ref.dtype)
            for i in range(pencils):
                o_ref[0, i % 2, 0, i // 2] = total[i * rows : (i + 1) * rows]

        def slabs(j):
            pltpu.emit_pipeline(
                slab, grid=(lines // group,), in_specs=[slab_spec, mask_spec], out_specs=[slab_spec]
            )(mid_ref.at[j], mask_ref, vol_ref.at[j])

        for j in range(last):
            for i in range(len(shifts)):
                moves[j][i].wait_send()
                if j + 1 < last:
                    moves[j + 1][i].start()
                else:
                    ends[0][i].start()
                    ends[1][i].start()
            for copy in moves[j]:
                copy.wait_recv()
            own[j].wait()
            pltpu.emit_pipeline(
                forward, grid=(slices,), in_specs=[plane, image_spec], out_specs=[plane]
            )(out_ref.at[j], full_ref, mid_ref.at[j])
            slabs(j)
            pltpu.emit_pipeline(
                backward, grid=(share, columns), in_specs=[strided, strided], out_specs=[part_spec]
            )(vol_ref.at[j], out_ref.at[j], part_ref.at[j])
        own[last].wait()
        for g in range(pieces):
            for i in range(len(shifts)):
                ends[g][i].wait_send()
                if g + 2 < pieces:
                    ends[g + 2][i].start()
            for copy in ends[g]:
                copy.wait_recv()
            piece = pl.ds(g * run, run)
            pltpu.emit_pipeline(
                forward, grid=(run,), in_specs=[plane, image_spec], out_specs=[plane]
            )(out_ref.at[last, piece], full_ref.at[:, piece], mid_ref.at[last, piece])
        slabs(last)

    dma = pltpu.SemaphoreType.DMA
    anywhere = pl.BlockSpec(memory_space=pl.ANY)
    vmem = pl.BlockSpec(memory_space=pltpu.VMEM)
    whole = jax.ShapeDtypeStruct((per, slices, lines, width), jnp.bfloat16)
    return pl.pallas_call(
        kernel,
        out_shape=[
            whole,
            jax.ShapeDtypeStruct((2, slices, chips, rows, width), jnp.bfloat16),
            whole,
            whole,
            jax.ShapeDtypeStruct((last, share, 2, columns, chips, rows, width), jnp.bfloat16),
        ],
        in_specs=[anywhere] * 3 + [vmem] * 6,
        out_specs=[anywhere] * 5,
        scratch_shapes=[
            dma((per + 1,)),
            dma((last, pencils - 1)),
            dma((last, pencils - 1)),
            dma((pieces, pencils - 1)),
            dma((pieces, pencils - 1)),
            dma((chips - 1,)),
            dma((chips - 1,)),
            dma((columns - 1,)),
            dma((columns - 1,)),
            dma,
            dma,
        ],
        compiler_params=pltpu.CompilerParams(
            collective_id=0, has_side_effects=True, vmem_limit_bytes=56 << 20
        ),
        name="exchange_forward",
    )(coil_maps, object_image, mask, *tables)


def combine_call(volume, maps, parts, x_inv, y_inv):
    pencils, columns = lax.axis_size("pencil"), lax.axis_size("coil")
    per, slices, lines, width = volume.shape
    rows, chips, share, last = lines // pencils, pencils // 2, slices // columns, per - 1
    volume = volume.reshape(per, columns, share, lines, width)
    maps = maps.reshape(per, columns, share, lines, width)

    def kernel(
        vol_ref, map_ref, early_ref, xi_ref, yi_ref, part_ref, out_ref,
        mine, from_core, from_first, from_second, column_sum, from_chip,
        own_sem, core_send, core_recv, one_send, one_recv, two_send, two_recv, chip_send, chip_recv,
    ):
        me, column = lax.axis_index("pencil"), lax.axis_index("coil")
        chip, core = me // 2, me % 2

        barrier = pltpu.get_barrier_semaphore()
        pl.semaphore_signal(barrier, device_id=(column, me + 1 - 2 * core), device_id_type=MESH)
        for bit in (1, 2):
            pl.semaphore_signal(barrier, device_id=(flip(column, bit), me), device_id_type=MESH)
        for s in range(1, chips):
            pl.semaphore_signal(
                barrier, device_id=(column, lax.rem(me + 2 * s, pencils)), device_id_type=MESH
            )
        pl.semaphore_wait(barrier, chips + 2)

        def own_copy(k):
            return pltpu.make_async_copy(part_ref.at[k, core], mine.at[k], own_sem.at[k])

        def core_copy(k):
            return pltpu.make_async_remote_copy(
                src_ref=part_ref.at[k, 1 - core],
                dst_ref=from_core.at[k],
                send_sem=core_send.at[k],
                recv_sem=core_recv.at[k],
                device_id=(column, me + 1 - 2 * core),
                device_id_type=MESH,
            )

        side = [pl.ds(h * (chips // 2), chips // 2) for h in range(2)]

        def one_copy(k, h, n):
            target = flip(column, 1 + h)
            return pltpu.make_async_remote_copy(
                src_ref=mine.at[k, flip(column, 3) if n else target, side[h]],
                dst_ref=from_first.at[k, h, n],
                send_sem=one_send.at[k, 2 * h + n],
                recv_sem=one_recv.at[k, 2 * h + n],
                device_id=(target, me),
                device_id_type=MESH,
            )

        def two_copy(k, h):
            target = flip(column, 2 - h)
            return pltpu.make_async_remote_copy(
                src_ref=mine.at[k, target, side[h]],
                dst_ref=from_second.at[k, h],
                send_sem=two_send.at[k, h],
                recv_sem=two_recv.at[k, h],
                device_id=(target, me),
                device_id_type=MESH,
            )

        def chip_copy(k, s):
            target = lax.rem(chip + s, chips)
            return pltpu.make_async_remote_copy(
                src_ref=column_sum.at[k, target],
                dst_ref=from_chip.at[k, s - 1],
                send_sem=chip_send.at[k, s - 1],
                recv_sem=chip_recv.at[k, s - 1],
                device_id=(column, 2 * target + core),
                device_id_type=MESH,
            )

        def add(one, other):
            return (one.astype(jnp.float32) + other.astype(jnp.float32)).astype(jnp.bfloat16)

        def backward(block, map_block, early, o_ref):
            total = backward_body(block[0], map_block[0], xi_ref, yi_ref)
            for i in range(pencils):
                block_sum = total[i * rows : (i + 1) * rows]
                for j in range(last):
                    block_sum += early[j, i % 2, 0, i // 2].astype(jnp.float32)
                o_ref[i % 2, 0, i // 2] = block_sum.astype(o_ref.dtype)

        plane = pl.BlockSpec((1, lines, width), lambda c: (c, 0, 0))
        early_spec = pl.BlockSpec((last, 2, 1, chips, rows, width), lambda c: (0, 0, c, 0, 0, 0))
        part_spec = pl.BlockSpec((2, 1, chips, rows, width), lambda c: (0, c, 0, 0, 0))

        def step(t, carry):
            @pl.when(t < share)
            def _():
                pltpu.emit_pipeline(
                    backward,
                    grid=(columns,),
                    in_specs=[plane, plane, early_spec],
                    out_specs=[part_spec],
                )(
                    vol_ref.at[last, :, t], map_ref.at[last, :, t], early_ref.at[:, t],
                    part_ref.at[t],
                )
                core_copy(t).start()
                own_copy(t).start()

            @pl.when((t >= 1) & (t < share + 1))
            def _():
                k = t - 1
                own_copy(k).wait()
                core_copy(k).wait_recv()
                for c in range(columns):
                    for z in range(chips):
                        mine[k, c, z] = add(mine[k, c, z], from_core[k, c, z])
                for h in range(2):
                    for n in range(2):
                        one_copy(k, h, n).start()

            @pl.when((t >= 2) & (t < share + 2))
            def _():
                k = t - 2
                for h in range(2):
                    other = flip(column, 2 - h)
                    for n in range(2):
                        one_copy(k, h, n).wait_recv()
                    mine[k, other, side[h]] = add(mine[k, other, side[h]], from_first[k, h, 1])
                    two_copy(k, h).start()
                    mine[k, column, side[h]] = add(mine[k, column, side[h]], from_first[k, h, 0])

            @pl.when((t >= 3) & (t < share + 3))
            def _():
                k = t - 3
                for h in range(2):
                    two_copy(k, h).wait_recv()
                    column_sum[k, side[h]] = add(mine[k, column, side[h]], from_second[k, h])
                for s in range(1, chips):
                    chip_copy(k, s).start()

            @pl.when(t >= 4)
            def _():
                k = t - 4
                for s in range(1, chips):
                    chip_copy(k, s).wait_recv()
                total = column_sum[k, chip].astype(jnp.float32)
                for s in range(1, chips):
                    total += from_chip[k, s - 1].astype(jnp.float32)
                out_ref[k] = total

            return carry

        lax.fori_loop(0, share + 4, step, 0)

        def finish(k, carry):
            core_copy(k).wait_send()
            for h in range(2):
                for n in range(2):
                    one_copy(k, h, n).wait_send()
                two_copy(k, h).wait_send()
            for s in range(1, chips):
                chip_copy(k, s).wait_send()
            return carry

        lax.fori_loop(0, share, finish, 0)

    dma = pltpu.SemaphoreType.DMA
    anywhere = pl.BlockSpec(memory_space=pl.ANY)
    vmem = pl.BlockSpec(memory_space=pltpu.VMEM)
    block = (chips, rows, width)
    return pl.pallas_call(
        kernel,
        out_shape=[
            jax.ShapeDtypeStruct((share, 2, columns) + block, jnp.bfloat16),
            jax.ShapeDtypeStruct((share, rows, width), jnp.float32),
        ],
        in_specs=[anywhere, anywhere, anywhere, vmem, vmem],
        out_specs=[anywhere, vmem],
        scratch_shapes=[
            pltpu.VMEM((share, columns) + block, jnp.bfloat16),
            pltpu.VMEM((share, columns) + block, jnp.bfloat16),
            pltpu.VMEM((share, 2, 2, chips // 2, rows, width), jnp.bfloat16),
            pltpu.VMEM((share, 2, chips // 2, rows, width), jnp.bfloat16),
            pltpu.VMEM((share,) + block, jnp.bfloat16),
            pltpu.VMEM((share, chips - 1, rows, width), jnp.bfloat16),
            dma((share,)),
            dma((share,)),
            dma((share,)),
            dma((share, 4)),
            dma((share, 4)),
            dma((share, 2)),
            dma((share, 2)),
            dma((share, chips - 1)),
            dma((share, chips - 1)),
        ],
        compiler_params=pltpu.CompilerParams(
            collective_id=1, has_side_effects=True, vmem_limit_bytes=60 << 20
        ),
        name="backward_combine",
    )(volume, maps, parts, x_inv, y_inv)[1]


def plan_mask(sample_mask, readout):
    slices, lines, segments = sample_mask.shape
    run = readout // segments // 4
    flags = sample_mask.reshape(slices // 2, 2, lines // 2, 2, segments).transpose(1, 0, 3, 2, 4)
    flags = (flags > 0).astype(jnp.bfloat16).reshape(2, slices // 2, lines, segments)
    return jnp.repeat(flags, run, axis=3)


def whole_coils(object_image, coil_maps, sample_mask):
    readout = object_image.shape[2] // 2
    slices = object_image.shape[0]
    lines = object_image.shape[1] * lax.axis_size("pencil")
    group = 16
    tables = plan_tables(slices, lines, readout, group)
    mask = plan_mask(sample_mask, readout)
    maps, _, _, volume, parts = exchange_call(coil_maps, object_image, mask, tables, group, 4)
    return combine_call(volume, maps, parts, tables[1], tables[3])


def solution(mesh):
    placed = (P(None, "pencil", None), P("coil", None, "pencil", None), P())

    def on_device(object_image, coil_maps, sample_mask):
        pencils = lax.axis_size("pencil")
        whole = coil_maps.shape[0] % pencils == 0 and coil_maps.shape[0] >= 2 * pencils
        whole = whole and pencils >= 4 and pencils & (pencils - 1) == 0
        whole = whole and lax.axis_size("coil") == 4
        return (whole_coils if whole else split_lines)(object_image, coil_maps, sample_mask)

    return jax.shard_map(
        on_device, mesh=mesh, in_specs=placed, out_specs=P("coil", "pencil", None), check_vma=False
    )
```
